32 devices in a mesh: lon: 8 (over z, x), lat: 4 (over y, core).
Axes of the slice: x: 2, y: 2, z: 4, core: 2. Of those that a mesh axis runs over, the one named last changes fastest.
Arguments:
- sounding_kernel: float32 [72, 32768], P(None, ('lon', 'lat')), may hold values from 0.2 to 1.4
- sounding_misfit: float32 [32768], P(('lon', 'lat')), may hold values from -6 to 6
- sounding_owner: int32 [32768, 1], P(('lon', 'lat')), may hold values from 0 to 31; in each aligned block of 1024 rows (0 to 1023, 1024 to 2047, ...) at most 48 rows name the same one
- sounding_cell: int32 [32768], P(('lon', 'lat')), may hold values from 0 to 1023
- sounding_step: int32 [32768], P(('lon', 'lat')), may hold values from 0 to 1
- sounding_count: int32 [32], P(('lon', 'lat')), may hold values from 512 to 1024, as said below
- courant_x: float32 [72, 32, 1024], P(None, 'lat', 'lon'), may hold values from -0.45 to 0.45
- courant_y: float32 [72, 32, 1024], P(None, 'lat', 'lon'), may hold values from -0.45 to 0.45
- diffusivity: float32 [72, 32, 1024], P(None, 'lat', 'lon'), may hold values from 0.05 to 3000
- region_map: int32 [32, 1024], P('lat', 'lon'), may hold values from 0 to 4095, as said below
- region_owner: int32 [4096], replicated, may hold values from 0 to 4095, as said below
Outputs:
- adjoint_field: float32 [72, 32, 1024], P(None, 'lat', 'lon')
- region_sensitivity: float32 [2, 4096], P(None, ('lon', 'lat'))
The draws below stay inside these ranges and needn't reach their ends.
Inputs may be any that keep to these rules, and one draw needn't show every extreme that they name: `sounding_owner`: at most 48 soundings of one device name one owner, and some device sends exactly 48 to some owner. Only the first sounding_count slots of a device hold real soundings; some device has all 1024. `region_map`: of one device's columns, at most 64 lie in regions whose positions share one owner, and every device has exactly 64 columns for some owner. `region_owner`: each position is taken by exactly one region.
All inputs are finite; a program needn't handle non-finite values.
Results may differ from the reference program's by a relative error of at most 0.0003.
Values sent between devices are 32-bit elements; how exact they have to be, the bound alone decides.
A program may use at most 128 MiB of HBM per device.

```python
import math
import jax
import jax.numpy as jnp
import numpy as np
from jax import lax

LEV = 72
CLAT = 8
CLON = 128
STEPS = 2
S_DEV = 1024
REG_DEV = 128
CAP = 48
RCAP = 64
NLAT = 32
NLON = 1024
SOUNDINGS = 32768
REGIONS = 4096
N_LON = 8
N_LAT = 4
DEVICES = 32


def region_order(key):
    return jax.random.permutation(key, REGIONS).astype(jnp.int32)


def draw_sounding_count(key, part):
    key = jax.random.fold_in(key, 11)
    first, second = jax.random.split(key)
    counts = jax.random.randint(first, (DEVICES,), S_DEV // 2, S_DEV + 1)
    fullest = jax.random.randint(second, (), 0, DEVICES)
    return jnp.where(jnp.arange(DEVICES) == fullest, S_DEV, counts).astype(jnp.int32)


def draw_region_owner(key, part):
    return region_order(key)


def draw_region_map(key, part):
    ordering = region_order(key)
    inverse = jnp.argsort(ordering, stable=True).astype(jnp.int32)
    key = jax.random.fold_in(key, 21)
    columns = CLAT * CLON

    def one_device(device):
        sub = jax.random.fold_in(key, device)
        first, second, third, fourth = jax.random.split(sub, 4)
        home = jax.random.randint(first, (), 0, DEVICES).astype(jnp.int32)
        spread = jax.random.permutation(second, (DEVICES - 1) * RCAP)[:columns - RCAP].astype(jnp.int32) // RCAP
        others = (home + 1 + spread) % DEVICES
        owners = jnp.concatenate([jnp.full((RCAP,), home, jnp.int32), others.astype(jnp.int32)])
        owners = owners[jax.random.permutation(third, columns)]
        local = jax.random.randint(fourth, (columns,), 0, REG_DEV).astype(jnp.int32)
        return inverse[owners * REG_DEV + local]
    blocks = jax.vmap(one_device)(jnp.arange(DEVICES, dtype=jnp.int32))
    blocks = blocks.reshape(N_LON, N_LAT, CLAT, CLON).transpose(1, 2, 0, 3)
    return blocks.reshape(NLAT, NLON).astype(jnp.int32)


def log_between(key, shape, lower, upper):
    level = jax.random.uniform(key, shape, jnp.float32, jnp.log(lower), jnp.log(upper))
    return jnp.exp(level)


def draw_diffusivity(key, part):
    key = jax.random.fold_in(key, 31)
    first, second, third = jax.random.split(key, 3)
    shape = (LEV, NLAT, NLON)
    drawn = log_between(second, shape, 0.05, 3.0)
    mixed = jax.random.bernoulli(first, 0.5, (1, NLAT, NLON))
    strong = log_between(third, shape, 100.0, 2000.0)
    return jnp.where(mixed, strong, drawn).astype(jnp.float32)


def set_ends(array, stream_key, least, high):
    dims = array.shape
    index_at = [jax.random.randint(jax.random.fold_in(stream_key, axis), (), 0, dims[axis]) for axis in range(len(dims))]
    array = array.at[tuple(index_at)].set(least)
    longest = dims.index(max(dims))
    index_at[longest] = (index_at[longest] + 1) % dims[longest]
    return array.at[tuple(index_at)].set(high)


def level_of(rng, dims, shards, low, largest):
    level, own = 1.0, jax.random.fold_in(rng, 6)
    for axis_at, shards_of in shards:
        heights = jnp.exp(jax.random.uniform(jax.random.fold_in(own, axis_at), (shards_of,), jnp.float32, low / len(shards), largest / len(shards)))
        level = level * jnp.repeat(heights, dims[axis_at] // shards_of).reshape([-1 if axis == axis_at else 1 for axis in range(len(dims))])
    return level


def deal_out(own_key, own, number, rows, amount, top, limit, lean):
    ranking = jax.random.permutation(own_key, amount)
    packed, common = load_shares(amount, rows * top, limit, lean, True), load_shares(amount, rows * top, limit, lean, False)
    places = jnp.arange(amount)

    def named(tallies, rotation):
        used = int((tallies > 0).sum())
        fixed = max(1, used // 4)
        passed = fixed + (places - fixed + rotation * (used - fixed)) % max(1, amount - fixed)
        return jnp.zeros((amount,), jnp.int32).at[ranking[jnp.where(places < fixed, places, passed)]].set(jnp.asarray(tallies, jnp.int32))

    tallies = jnp.where(number % 4 == 0, named(packed, number // 4), named(common, number - number // 4 - 1))
    mixed = jax.random.permutation(jax.random.fold_in(own, 3), amount)
    giver, receiver = mixed[0:amount // 2 * 2:2], mixed[1:amount // 2 * 2:2]
    slack = jnp.minimum(tallies[giver] - 1, limit - tallies[receiver]) // 2
    slack = jnp.where((giver == ranking[0]) | (receiver == ranking[0]) | (tallies[receiver] == 0), 0, jnp.maximum(slack, 0))
    passed = jax.random.randint(jax.random.fold_in(own, 4), (amount // 2,), 0, 1 << 20) % (slack + 1)
    tallies = tallies.at[giver].add(-passed).at[receiver].add(passed)
    labels = jnp.searchsorted(jnp.cumsum(tallies), jnp.arange(rows * top), side="right").astype(jnp.int32)
    listing = labels.reshape(top, rows).T
    listing = listing[jax.random.permutation(jax.random.fold_in(own, 1), rows)]
    rotation = jax.random.randint(jax.random.fold_in(own, 2), (rows, 1), 0, top)
    return jnp.take_along_axis(listing, (jnp.arange(top)[None, :] + rotation) % top, axis=1)


def load_shares(count, total, reach, skew, full):
    loads = [(1 << 20) // math.isqrt(rank ** skew) + 1 for rank in range(1, count + 1)]
    largest = reach if full else min(reach, max(-(-total // count), total * loads[0] // sum(loads)))
    least = 1 if total - largest >= count - 1 else 0
    holding, spare = [largest] + [least] * (count - 1), total - largest - least * (count - 1)
    while spare > 0:
        movable = [i for i in range(1, count) if holding[i] < largest] or [i for i in range(1, count) if holding[i] < reach]
        whole, remaining = sum([loads[i] for i in movable]), spare
        for i in movable:
            more = min(reach - holding[i], max(1, remaining * loads[i] // whole), spare)
            holding[i] = holding[i] + more
            spare = spare - more
    return np.array(holding)


def gaussian(rng, shape, width, limit, pieces=(), kind=jnp.bfloat16):
    loudness = level_of(rng, shape, pieces, -0.22, 0.18) if pieces else 1.0
    entries = jax.random.normal(rng, shape, jnp.float32) * width * loudness
    return jnp.minimum(jnp.maximum(entries, -limit), limit).astype(kind)


def setup_inputs(seed: int = 0) -> dict:
    seeds = jax.random.split(jax.random.key(seed), 12)
    sounding_kernel = jnp.clip(0.2 + 1.19999997 * jax.random.uniform(seeds[0], (LEV, SOUNDINGS), jnp.float32) ** level_of(seeds[0], (LEV, SOUNDINGS), ((1, 32),), -0.2, 0.2), 0.2, 1.4)
    sounding_misfit = gaussian(seeds[1], (SOUNDINGS,), 1.0, 6.0, ((0, 32),), jnp.float32)
    sounding_owner_keys = jax.random.split(jax.random.fold_in(seeds[2], 1), SOUNDINGS // S_DEV)
    sounding_owner_turns = jax.random.permutation(jax.random.fold_in(seeds[2], 3), SOUNDINGS // S_DEV)
    sounding_owner = jax.vmap(lambda own, number: deal_out(jax.random.fold_in(seeds[2], 2), own, number, S_DEV, DEVICES, 1, CAP, 2))(sounding_owner_keys, sounding_owner_turns).reshape((SOUNDINGS, 1))
    sounding_cell = set_ends(jax.random.randint(seeds[3], (SOUNDINGS,), 0, CLAT * CLON), jax.random.fold_in(seeds[3], 1), 0, (CLAT * CLON) - 1).astype(jnp.int32)
    sounding_step = set_ends(jax.random.randint(seeds[4], (SOUNDINGS,), 0, STEPS), jax.random.fold_in(seeds[4], 1), 0, STEPS - 1).astype(jnp.int32)
    sounding_count = draw_sounding_count(jax.random.fold_in(seeds[11], 71), 0)
    courant_x = jnp.clip(jax.random.uniform(seeds[6], (LEV, NLAT, NLON), jnp.float32, -0.45, 0.45) * level_of(seeds[6], (LEV, NLAT, NLON), ((1, 4), (2, 8)), -0.4, 0.0), -0.45, 0.45)
    courant_y = jnp.clip(jax.random.uniform(seeds[7], (LEV, NLAT, NLON), jnp.float32, -0.45, 0.45) * level_of(seeds[7], (LEV, NLAT, NLON), ((1, 4), (2, 8)), -0.4, 0.0), -0.45, 0.45)
    diffusivity = draw_diffusivity(jax.random.fold_in(seeds[11], 71), 0)
    region_map = draw_region_map(jax.random.fold_in(seeds[11], 71), 0)
    region_owner = draw_region_owner(jax.random.fold_in(seeds[11], 71), 0)
    return {"sounding_kernel": sounding_kernel, "sounding_misfit": sounding_misfit, "sounding_owner": sounding_owner, "sounding_cell": sounding_cell, "sounding_step": sounding_step, "sounding_count": sounding_count, "courant_x": courant_x, "courant_y": courant_y, "diffusivity": diffusivity, "region_map": region_map, "region_owner": region_owner}


def advect_global(field, courant_x, courant_y):
    west = jnp.roll(field, 1, axis=2)
    east = jnp.roll(field, -1, axis=2)
    south = jnp.pad(field, ((0, 0), (1, 0), (0, 0)))[:, :-1, :]
    north = jnp.pad(field, ((0, 0), (0, 1), (0, 0)))[:, 1:, :]
    return (field - jnp.maximum(courant_x, 0.0) * (field - west)
            - jnp.maximum(-courant_x, 0.0) * (field - east)
            - jnp.maximum(courant_y, 0.0) * (field - south)
            - jnp.maximum(-courant_y, 0.0) * (field - north))


def diffuse(field, coupling):
    below = jnp.concatenate([jnp.zeros_like(coupling[:1]), coupling[:-1]], axis=0)
    middle = 1.0 + below + coupling

    def forward(carry, item):
        w_prev, g_prev = carry
        low, mid, upper, rhs = item
        denom = mid + low * w_prev
        w_now = -upper / denom
        g_now = (rhs + low * g_prev) / denom
        return (w_now, g_now), (w_now, g_now)

    zero = jnp.zeros_like(field[0])
    _, (w_all, g_all) = lax.scan(forward, (zero, zero), (below, middle, coupling, field))

    def backward(x_next, item):
        w_now, g_now = item
        x_now = g_now - w_now * x_next
        return x_now, x_now

    _, solved = lax.scan(backward, zero, (w_all, g_all), reverse=True)
    return solved


def reference(sounding_kernel, sounding_misfit, sounding_owner, sounding_cell, sounding_step,
              sounding_count, courant_x, courant_y, diffusivity, region_map, region_owner):
    lat_cells = CLAT * N_LAT
    lon_cells = CLON * N_LON
    total = lat_cells * lon_cells
    order = jnp.arange(SOUNDINGS, dtype=jnp.int32)
    valid = (order % S_DEV) < sounding_count[order // S_DEV]
    owner = sounding_owner[:, 0]
    glat = (owner % N_LAT) * CLAT + sounding_cell // CLON
    glon = (owner // N_LAT) * CLON + sounding_cell % CLON
    target = (glat * lon_cells + glon).astype(jnp.int32)
    weight = jnp.where(valid, sounding_misfit, jnp.zeros_like(sounding_misfit))
    forcing = sounding_kernel.T * weight[:, None]
    positions = region_owner[region_map].reshape(-1)
    field = jnp.zeros((LEV, lat_cells, lon_cells), jnp.float32)
    sums = []
    for step in range(STEPS):
        ids = jnp.where(sounding_step == step, target, total).astype(jnp.int32)
        deposit = jax.ops.segment_sum(forcing, ids, num_segments=total + 1)[:total]
        field = field + deposit.T.reshape(LEV, lat_cells, lon_cells)
        field = diffuse(advect_global(field, courant_x, courant_y), diffusivity)
        sums.append(jax.ops.segment_sum(field[0].reshape(-1), positions, num_segments=REGIONS))
    return field, jnp.stack(sums)
```

```python
import functools

import jax
import jax.numpy as jnp
from jax import lax
from jax.experimental import pallas as pl
from jax.experimental.pallas import tpu as pltpu
from jax.sharding import PartitionSpec as P

STEPS = 2


def with_halo(x, sides, width):
    for axis, dim in sides:
        size, length = (lax.axis_size(axis), x.shape[dim])
        up = [(i, (i + 1) % size) for i in range(size)]
        down = [(j, i) for i, j in up]
        last = lax.slice_in_dim(x, length - width, length, axis=dim)
        leading = lax.slice_in_dim(x, 0, width, axis=dim)
        before = lax.ppermute(last, axis, up)
        after = lax.ppermute(leading, axis, down)
        x = jnp.concatenate([before, x, after], axis=dim)
    return x


def advect(padded, courant_x, courant_y):
    center = padded[:, 1:-1, 1:-1]
    west = padded[:, 1:-1, :-2]
    east = padded[:, 1:-1, 2:]
    south = padded[:, :-2, 1:-1]
    north = padded[:, 2:, 1:-1]
    return (
        center
        - jnp.maximum(courant_x, 0.0) * (center - west)
        - jnp.maximum(-courant_x, 0.0) * (center - east)
        - jnp.maximum(courant_y, 0.0) * (center - south)
        - jnp.maximum(-courant_y, 0.0) * (center - north)
    )


def diffuse(field, coupling):
    below = jnp.concatenate([jnp.zeros_like(coupling[:1]), coupling[:-1]], axis=0)
    middle = 1.0 + below + coupling

    def forward(carry, item):
        w_prev, g_prev = carry
        low, mid, upper, rhs = item
        denom = mid + low * w_prev
        w_now = -upper / denom
        g_now = (rhs + low * g_prev) / denom
        return ((w_now, g_now), (w_now, g_now))

    zero = jnp.zeros_like(field[0])
    _, (w_all, g_all) = lax.scan(forward, (zero, zero), (below, middle, coupling, field))

    def backward(x_next, item):
        w_now, g_now = item
        x_now = g_now - w_now * x_next
        return (x_now, x_now)

    _, solved = lax.scan(backward, zero, (w_all, g_all), reverse=True)
    return solved


def lat_mask(rows_lat, width):
    first = lax.axis_index("lat") * rows_lat - width
    inside = first + jnp.arange(rows_lat + 2 * width, dtype=jnp.int32)
    limit = rows_lat * lax.axis_size("lat")
    return ((inside >= 0) & (inside < limit)).astype(jnp.float32)[:, None]


def general_body(
    sounding_kernel,
    sounding_misfit,
    sounding_owner,
    sounding_cell,
    sounding_step,
    sounding_count,
    courant_x,
    courant_y,
    diffusivity,
    region_map,
    region_owner,
):
    levels, rows_lat, rows_lon = courant_x.shape
    cells = rows_lat * rows_lon
    lon_count = lax.axis_size("lon")
    lat_count = lax.axis_size("lat")
    devices = lon_count * lat_count
    per_device = sounding_misfit.shape[0]
    capacity = max(2, 3 * per_device // (2 * devices))
    regions = region_owner.shape[0]
    slots = jnp.arange(per_device, dtype=jnp.int32)
    valid = slots < sounding_count[0]
    owner = sounding_owner[:, 0]
    earlier = (
        (owner[:, None] == owner[None, :]) & (slots[:, None] < slots[None, :]) & valid[:, None]
    )
    rank = jnp.sum(earlier.astype(jnp.int32), axis=0)
    spill = devices * capacity
    target = jnp.where(valid, owner * capacity + rank, spill)
    forcing = sounding_misfit[:, None] * sounding_kernel.T
    code = (sounding_step * cells + sounding_cell).astype(jnp.float32)
    send_rows = jax.ops.segment_sum(forcing, target, num_segments=spill + 1)[:spill]
    send_code = jax.ops.segment_sum(code, target, num_segments=spill + 1)[:spill]
    send_rows = send_rows.reshape(lon_count, lat_count, capacity * levels)
    send_code = send_code.reshape(lon_count, lat_count, capacity)
    got_rows, got_code = (
        lax.all_to_all(
            lax.all_to_all(send_rows, "lon", split_axis=0, concat_axis=0, tiled=True),
            "lat",
            split_axis=1,
            concat_axis=1,
            tiled=True,
        ),
        lax.all_to_all(
            lax.all_to_all(send_code, "lon", split_axis=0, concat_axis=0, tiled=True),
            "lat",
            split_axis=1,
            concat_axis=1,
            tiled=True,
        ),
    )
    got_rows = got_rows.reshape(devices * capacity, levels)
    got_code = got_code.reshape(-1).astype(jnp.int32)
    deposit = jax.ops.segment_sum(got_rows, got_code, num_segments=STEPS * cells)
    deposit = (
        deposit.reshape(STEPS, cells, levels)
        .transpose(0, 2, 1)
        .reshape(STEPS, levels, rows_lat, rows_lon)
    )
    field = jnp.zeros((levels, rows_lat, rows_lon), jnp.float32)
    surfaces = []
    for step in range(STEPS):
        field = field + deposit[step]
        padded = with_halo(field, (("lon", 2), ("lat", 1)), 1)
        padded = padded * lat_mask(rows_lat, 1)
        field = diffuse(advect(padded, courant_x, courant_y), diffusivity)
        surfaces.append(field[0])
    positions = region_owner[region_map].reshape(-1)

    def region_partial(surface):
        return jax.ops.segment_sum(surface.reshape(-1), positions, num_segments=regions)

    partial_all = jnp.stack([region_partial(surface) for surface in surfaces])
    totals = lax.psum_scatter(partial_all, ("lon", "lat"), scatter_dimension=1, tiled=True)
    return (field, totals)


MESH = pl.DeviceIdType.MESH
F32 = jnp.float32
BF16 = jnp.bfloat16
I32 = jnp.int32


def iota(shape, dim):
    return lax.broadcasted_iota(I32, shape, dim)


def one_hot(test, dtype=BF16):
    return jnp.where(test, 1.0, 0.0).astype(dtype)


def split(x):
    high = x.astype(BF16)
    return high, (x - high.astype(F32)).astype(BF16)


def dot_nt(a, b):
    return lax.dot_general(a, b, (((1,), (1,)), ((), ())), preferred_element_type=F32)


def kernel(
    lat_count,
    devices,
    sk_ref,
    misfit_ref,
    owner_ref,
    cell_ref,
    step_ref,
    count_ref,
    cx_ref,
    cy_ref,
    dif_ref,
    map_ref,
    table_ref,
    out_ref,
    reg_ref,
    target,
    weights,
    send,
    got,
    dep0,
    dep1,
    base,
    inv,
    low,
    up,
    lon_out,
    lon_in,
    lat_out,
    lat_in,
    own_hot,
    loc_hot,
    part,
    part_in,
    a2a_send,
    a2a_recv,
    halo_send,
    halo_recv,
    reg_send,
    reg_recv,
):
    levels = cx_ref.shape[0]
    blocks = levels // 8
    planes = devices // 8
    half = devices * 16
    lon = lax.axis_index("lon")
    lat = lax.axis_index("lat")
    lon_count = devices // lat_count
    me = lon * lat_count + lat
    plane = me // 8
    inner = me % 8

    def place(peer):
        return (peer // lat_count, peer % lat_count)

    def flip(value, mask, bits):
        total = 0
        for bit in range(bits):
            v = (value // (1 << bit)) % 2
            m = (mask // (1 << bit)) % 2
            total = total + (v + m - 2 * v * m) * (1 << bit)
        return total

    bits = devices.bit_length() - 1
    barrier = pltpu.get_barrier_semaphore()

    def greet(d, carry):
        peer = lax.rem(me + d, devices)
        pl.semaphore_signal(barrier, inc=1, device_id=place(peer), device_id_type=MESH)
        return carry

    lax.fori_loop(1, devices, greet, 0)

    lane1 = iota((1, 128), 1)
    owner_iota = iota((devices, 128), 0)
    hots, valids, owners = [], [], []
    count = count_ref[0]
    for c in range(8):
        valid = (lane1 + c * 128) < count
        row = owner_ref[c : c + 1, :]
        hots.append(one_hot(jnp.where(valid, row, -1) == owner_iota, F32))
        valids.append(valid)
        owners.append(row)
    earlier = one_hot((iota((128, 256), 0) < iota((128, 256), 1)))
    ranks = jnp.dot(
        jnp.concatenate(hots, axis=0).astype(BF16), earlier, preferred_element_type=F32
    )
    carry = jnp.zeros((devices, 128), F32)
    for c in range(8):
        part_c = ranks[c * devices : (c + 1) * devices]
        rank = jnp.sum(hots[c] * (part_c[:, :128] + carry), axis=0, keepdims=True).astype(I32)
        carry = carry + part_c[:, 128:]
        spot = (rank // 16) * half + owners[c] * 16 + rank % 16
        target[c : c + 1, :] = jnp.where(valids[c], spot, -1)

    for c in range(8):
        at = slice(c * 128, (c + 1) * 128)
        forcing = sk_ref[:, at] * misfit_ref[c : c + 1, :]
        code = (step_ref[c : c + 1, :] * 1024 + cell_ref[c : c + 1, :]).astype(F32)
        code = jnp.broadcast_to(code, (8, 128))
        for h in range(2):
            if h == 0:
                rest = forcing[:40]
            else:
                rest = jnp.concatenate([forcing[40:], jnp.zeros((8, 128), F32)], axis=0)
            high, small = split(jnp.concatenate([forcing, code, rest, code], axis=0))
            weights[h, 0:128, at] = high
            weights[h, 128:256, at] = small

    pl.semaphore_wait(barrier, devices - 1)

    sub128 = iota((128, 128), 0)
    lane128 = iota((128, 128), 1)
    order = [2, 3, 1, 0]

    def select_rows(first):
        return jnp.concatenate(
            [one_hot(target[c : c + 1, :] - first == sub128) for c in range(8)], axis=1
        )

    for x in order:
        there = flip(plane, x, bits - 3)
        rows = pl.ds(pl.multiple_of(there * 128, 128), 128)
        late = select_rows(2 * half + there * 128)
        for h in range(2):
            picks = jnp.concatenate([select_rows(h * half + there * 128), late], axis=0)
            both = dot_nt(picks, weights[h])
            both = both[:, :128] + both[:, 128:]
            send[h, rows, :] = jnp.where(lane128 < 80, both[:128], both[128:])

        def ship(e, carry, x=x):
            peer = flip(plane, x, bits - 3) * 8 + flip(inner, e, 3)
            pltpu.make_async_remote_copy(
                src_ref=send.at[:, pl.ds(pl.multiple_of(peer * 16, 16), 16), :],
                dst_ref=got.at[:, pl.ds(pl.multiple_of(me * 16, 16), 16), :],
                send_sem=a2a_send.at[x],
                recv_sem=a2a_recv.at[x],
                device_id=place(peer),
                device_id_type=MESH,
            ).start()
            return carry

        lax.fori_loop(1 if x == 0 else 0, 8, ship, 0)
    mine = pl.ds(pl.multiple_of(me * 16, 16), 16)
    got[:, mine, :] = send[:, mine, :]

    def factor(b, carry):
        k_prev, up_prev = carry
        for i in range(8):
            row = pl.ds(pl.multiple_of(b * 64 + i * 8, 8), 8)
            k_now = dif_ref[b * 8 + i]
            r = 1.0 / ((1.0 + k_prev + k_now) - k_prev * up_prev)
            inv[row, :] = r
            low[row, :] = k_prev * r
            up_prev = k_now * r
            up[row, :] = up_prev
            k_prev = k_now
        return (k_prev, up_prev)

    zero = jnp.zeros((8, 128), F32)
    lax.fori_loop(0, blocks, factor, (zero, zero))

    table = table_ref[...]
    table = jnp.concatenate([table // 128, table % 128], axis=0).astype(F32).astype(BF16)
    for a in range(8):
        at = slice(a * 128, (a + 1) * 128)
        region = map_ref[a : a + 1, :]
        found = jnp.dot(table, one_hot(region % 128 == sub128), preferred_element_type=F32)
        pick = one_hot(region // 128 == owner_iota, F32)
        own = jnp.sum(found[:devices] * pick, axis=0, keepdims=True).astype(I32)
        loc = jnp.sum(found[devices:] * pick, axis=0, keepdims=True).astype(I32)
        own_hot[:, at] = one_hot(own == owner_iota, F32)
        loc_hot[:, at] = one_hot(loc == sub128)

    sub8 = iota((8, 128), 0)
    lane256 = iota((128, 256), 1)

    def spread(rows, code):
        mask = one_hot((code // 128) % 8 == sub8, F32)
        y = (rows[:, None, :] * mask[None]).reshape(levels * 8, 128)
        return split(y)

    def column(code):
        return one_hot(code % 128 + (code // 1024) * 128 == lane256)

    for n, x in enumerate(order):
        there = flip(plane, x, bits - 3)
        if x == 0:
            seen = got.at[:, pl.ds(0, 112), :]
        else:
            seen = got.at[:, pl.ds(0, 128), :]
        pltpu.make_async_copy(seen, seen, a2a_recv.at[x]).wait()
        rows = pl.ds(pl.multiple_of(there * 128, 128), 128)
        first = got[0, rows, :]
        second = got[1, rows, :]
        first_t = first.T
        second_t = second.T
        late_t = jnp.concatenate([first_t[80:120], second_t[80:112]], axis=0)
        left, right = [], []
        for values, code_row, code_col in (
            (first_t[:72], first_t[72:73], first[:, 72:73]),
            (second_t[:72], second_t[72:73], second[:, 72:73]),
            (late_t, first_t[120:121], first[:, 120:121]),
        ):
            left.extend(spread(values, code_row.astype(I32)))
            right.extend([column(code_col.astype(I32))] * 2)
        total = jnp.dot(
            jnp.concatenate(left, axis=1),
            jnp.concatenate(right, axis=0),
            preferred_element_type=F32,
        )
        if n == 0:
            dep0[...] = total[:, :128]
            dep1[...] = total[:, 128:]
        else:
            dep0[...] += total[:, :128]
            dep1[...] += total[:, 128:]

    lane8 = iota((8, 128), 1)
    east = (lax.rem(lon + 1, lon_count), lat)
    west = (lax.rem(lon + lon_count - 1, lon_count), lat)
    north = (lon, lax.rem(lat + 1, lat_count))
    south = (lon, lax.rem(lat + lat_count - 1, lat_count))
    has_south = (lat > 0).astype(F32)
    has_north = (lat < lat_count - 1).astype(F32)

    def region_part(surface, step):
        spread_rows = jnp.concatenate(
            [own_hot[:, a * 128 : (a + 1) * 128] * surface[a : a + 1] for a in range(8)], axis=1
        )
        both = dot_nt(jnp.concatenate(split(spread_rows), axis=0), loc_hot[...])
        total = both[:devices] + both[devices:]
        for o in range(devices):
            part[o, step : step + 1, :] = total[o : o + 1]

    surface = None
    for step in range(STEPS):
        def gather(n, carry):
            first, last = carry
            b = blocks - 1 - n
            first = pltpu.roll(first, 8, 1)
            last = pltpu.roll(last, 8, 1)
            for i in range(8):
                x = dep0[pl.ds(pl.multiple_of(b * 64 + i * 8, 8), 8), :]
                first = jnp.where(lane8 == i, pltpu.roll(x, i, 1) if i else x, first)
                last = jnp.where(lane8 == i, pltpu.roll(x, i + 1, 1), last)
            return (first, last)

        first, last = lax.fori_loop(0, blocks, gather, (zero, zero))
        lon_out[step, 0] = first
        lon_out[step, 1] = last
        lat_out[step, 0] = dep0[pl.ds(0, levels, stride=8), :]
        lat_out[step, 1] = dep0[pl.ds(7, levels, stride=8), :]
        copies = []
        for n, (src, dst, to) in enumerate(
            (
                (lat_out.at[step, 0], lat_in.at[step, 1], south),
                (lat_out.at[step, 1], lat_in.at[step, 0], north),
                (lon_out.at[step, 0], lon_in.at[step, 1], west),
                (lon_out.at[step, 1], lon_in.at[step, 0], east),
            )
        ):
            copy = pltpu.make_async_remote_copy(
                src_ref=src,
                dst_ref=dst,
                send_sem=halo_send.at[step, n],
                recv_sem=halo_recv.at[step, n],
                device_id=to,
                device_id_type=MESH,
            )
            copy.start()
            copies.append(copy)

        def inside(b, carry):
            for i in range(8):
                row = pl.ds(pl.multiple_of(b * 64 + i * 8, 8), 8)
                x = dep0[row, :]
                cx = cx_ref[b * 8 + i]
                cy = cy_ref[b * 8 + i]
                to_west = jnp.where(lane8 == 0, 0.0, pltpu.roll(x, 1, 1))
                to_east = jnp.where(lane8 == 127, 0.0, pltpu.roll(x, 127, 1))
                to_south = jnp.where(sub8 == 0, 0.0, pltpu.roll(x, 1, 0))
                to_north = jnp.where(sub8 == 7, 0.0, pltpu.roll(x, 7, 0))
                base[row, :] = (
                    x
                    - jnp.maximum(cx, 0.0) * (x - to_west)
                    - jnp.maximum(-cx, 0.0) * (x - to_east)
                    - jnp.maximum(cy, 0.0) * (x - to_south)
                    - jnp.maximum(-cy, 0.0) * (x - to_north)
                )
            return carry

        lax.fori_loop(0, blocks, inside, 0)
        if step > 0:
            region_part(surface, step - 1)
        for copy in copies:
            copy.wait()

        def forward(b, carry):
            g, from_west, from_east = carry
            eight = pl.ds(pl.multiple_of(b * 8, 8), 8)
            from_south = lat_in[step, 0, eight, :] * has_south
            from_north = lat_in[step, 1, eight, :] * has_north
            for i in range(8):
                row = pl.ds(pl.multiple_of(b * 64 + i * 8, 8), 8)
                cx = cx_ref[b * 8 + i]
                cy = cy_ref[b * 8 + i]
                w = pltpu.roll(from_west, 128 - i, 1) if i else from_west
                e = pltpu.roll(from_east, 127 - i, 1)
                x_edge = jnp.where(
                    lane8 == 0,
                    jnp.maximum(cx, 0.0) * w,
                    jnp.where(lane8 == 127, jnp.maximum(-cx, 0.0) * e, 0.0),
                )
                y_edge = jnp.where(
                    sub8 == 0,
                    jnp.maximum(cy, 0.0) * from_south[i : i + 1],
                    jnp.where(sub8 == 7, jnp.maximum(-cy, 0.0) * from_north[i : i + 1], 0.0),
                )
                rhs = base[row, :] + x_edge + y_edge
                g = rhs * inv[row, :] + low[row, :] * g
                base[row, :] = g
            return (g, pltpu.roll(from_west, 120, 1), pltpu.roll(from_east, 120, 1))

        lax.fori_loop(0, blocks, forward, (zero, lon_in[step, 0], lon_in[step, 1]))

        def backward(n, x):
            b = blocks - 1 - n
            for i in reversed(range(8)):
                row = pl.ds(pl.multiple_of(b * 64 + i * 8, 8), 8)
                x = base[row, :] + up[row, :] * x
                if step < STEPS - 1:
                    dep0[row, :] = x + dep1[row, :]
                else:
                    out_ref[b * 8 + i] = x
            return x

        surface = lax.fori_loop(0, blocks, backward, zero)

    region_part(surface, STEPS - 1)

    def hand_out(d, carry):
        peer = lax.rem(me + d, devices)
        pltpu.make_async_remote_copy(
            src_ref=part.at[peer],
            dst_ref=part_in.at[me],
            send_sem=reg_send,
            recv_sem=reg_recv,
            device_id=place(peer),
            device_id_type=MESH,
        ).start()
        return carry

    lax.fori_loop(1, devices, hand_out, 0)
    part_in[me] = part[me]
    others = part_in.at[pl.ds(0, devices - 1)]
    pltpu.make_async_copy(others, others, reg_recv).wait()
    reg_ref[...] = jnp.sum(part_in[...], axis=0)

    others = part.at[pl.ds(0, devices - 1)]
    pltpu.make_async_copy(others, others, reg_send).wait()
    for x in order:
        seen = send.at[:, pl.ds(0, 112 if x == 0 else 128), :]
        pltpu.make_async_copy(seen, seen, a2a_send.at[x]).wait()


def body(
    sounding_kernel,
    sounding_misfit,
    sounding_owner,
    sounding_cell,
    sounding_step,
    sounding_count,
    courant_x,
    courant_y,
    diffusivity,
    region_map,
    region_owner,
):
    levels, rows_lat, rows_lon = courant_x.shape
    lat_count = lax.axis_size("lat")
    devices = lat_count * lax.axis_size("lon")
    per_device = sounding_misfit.shape[0]
    capacity = max(2, 3 * per_device // (2 * devices))
    if (capacity, devices, levels, rows_lat, rows_lon, per_device) != (48, 32, 72, 8, 128, 1024):
        return general_body(
            sounding_kernel,
            sounding_misfit,
            sounding_owner,
            sounding_cell,
            sounding_step,
            sounding_count,
            courant_x,
            courant_y,
            diffusivity,
            region_map,
            region_owner,
        )
    vmem = pl.BlockSpec(memory_space=pltpu.VMEM)
    smem = pl.BlockSpec(memory_space=pltpu.SMEM)
    cells = (levels * rows_lat, rows_lon)
    return pl.pallas_call(
        functools.partial(kernel, lat_count, devices),
        out_shape=(
            jax.ShapeDtypeStruct(courant_x.shape, F32),
            jax.ShapeDtypeStruct((STEPS, 128), F32),
        ),
        in_specs=[vmem] * 5 + [smem] + [vmem] * 5,
        out_specs=(vmem, vmem),
        scratch_shapes=[
            pltpu.VMEM((8, 128), I32),
            pltpu.VMEM((2, 256, per_device), BF16),
            pltpu.VMEM((2, devices * 16, 128), F32),
            pltpu.VMEM((2, devices * 16, 128), F32),
            pltpu.VMEM(cells, F32),
            pltpu.VMEM(cells, F32),
            pltpu.VMEM(cells, F32),
            pltpu.VMEM(cells, F32),
            pltpu.VMEM(cells, F32),
            pltpu.VMEM(cells, F32),
            pltpu.VMEM((STEPS, 2, 8, 128), F32),
            pltpu.VMEM((STEPS, 2, 8, 128), F32),
            pltpu.VMEM((STEPS, 2, levels, 128), F32),
            pltpu.VMEM((STEPS, 2, levels, 128), F32),
            pltpu.VMEM((devices, 1024), F32),
            pltpu.VMEM((128, 1024), BF16),
            pltpu.VMEM((devices, STEPS, 128), F32),
            pltpu.VMEM((devices, STEPS, 128), F32),
            pltpu.SemaphoreType.DMA((4,)),
            pltpu.SemaphoreType.DMA((4,)),
            pltpu.SemaphoreType.DMA((STEPS, 4)),
            pltpu.SemaphoreType.DMA((STEPS, 4)),
            pltpu.SemaphoreType.DMA,
            pltpu.SemaphoreType.DMA,
        ],
        compiler_params=pltpu.CompilerParams(
            collective_id=0, has_side_effects=True, vmem_limit_bytes=40 * 1024 * 1024
        ),
    )(
        sounding_kernel,
        sounding_misfit.reshape(8, 128),
        sounding_owner.reshape(8, 128),
        sounding_cell.reshape(8, 128),
        sounding_step.reshape(8, 128),
        sounding_count,
        courant_x,
        courant_y,
        diffusivity,
        region_map,
        region_owner.reshape(-1, 128),
    )


def solution(mesh):
    placed = (
        P(None, ("lon", "lat")),
        P(("lon", "lat")),
        P(("lon", "lat"), None),
        P(("lon", "lat")),
        P(("lon", "lat")),
        P(("lon", "lat")),
        P(None, "lat", "lon"),
        P(None, "lat", "lon"),
        P(None, "lat", "lon"),
        P("lat", "lon"),
        P(),
    )
    return jax.shard_map(
        body,
        mesh=mesh,
        in_specs=placed,
        out_specs=(P(None, "lat", "lon"), P(None, ("lon", "lat"))),
        check_vma=False,
    )
```

```python
import functools

import jax
import jax.numpy as jnp
from jax import lax
from jax.experimental import pallas as pl
from jax.experimental.pallas import tpu as pltpu
from jax.sharding import PartitionSpec as P

STEPS = 2


def with_halo(x, sides, width):
    for axis, dim in sides:
        size, length = (lax.axis_size(axis), x.shape[dim])
        up = [(i, (i + 1) % size) for i in range(size)]
        down = [(j, i) for i, j in up]
        last = lax.slice_in_dim(x, length - width, length, axis=dim)
        leading = lax.slice_in_dim(x, 0, width, axis=dim)
        before = lax.ppermute(last, axis, up)
        after = lax.ppermute(leading, axis, down)
        x = jnp.concatenate([before, x, after], axis=dim)
    return x


def advect(padded, courant_x, courant_y):
    center = padded[:, 1:-1, 1:-1]
    west = padded[:, 1:-1, :-2]
    east = padded[:, 1:-1, 2:]
    south = padded[:, :-2, 1:-1]
    north = padded[:, 2:, 1:-1]
    return (
        center
        - jnp.maximum(courant_x, 0.0) * (center - west)
        - jnp.maximum(-courant_x, 0.0) * (center - east)
        - jnp.maximum(courant_y, 0.0) * (center - south)
        - jnp.maximum(-courant_y, 0.0) * (center - north)
    )


def diffuse(field, coupling):
    below = jnp.concatenate([jnp.zeros_like(coupling[:1]), coupling[:-1]], axis=0)
    middle = 1.0 + below + coupling

    def forward(carry, item):
        w_prev, g_prev = carry
        low, mid, upper, rhs = item
        denom = mid + low * w_prev
        w_now = -upper / denom
        g_now = (rhs + low * g_prev) / denom
        return ((w_now, g_now), (w_now, g_now))

    zero = jnp.zeros_like(field[0])
    _, (w_all, g_all) = lax.scan(forward, (zero, zero), (below, middle, coupling, field))

    def backward(x_next, item):
        w_now, g_now = item
        x_now = g_now - w_now * x_next
        return (x_now, x_now)

    _, solved = lax.scan(backward, zero, (w_all, g_all), reverse=True)
    return solved


def lat_mask(rows_lat, width):
    first = lax.axis_index("lat") * rows_lat - width
    inside = first + jnp.arange(rows_lat + 2 * width, dtype=jnp.int32)
    limit = rows_lat * lax.axis_size("lat")
    return ((inside >= 0) & (inside < limit)).astype(jnp.float32)[:, None]


def general_body(
    sounding_kernel,
    sounding_misfit,
    sounding_owner,
    sounding_cell,
    sounding_step,
    sounding_count,
    courant_x,
    courant_y,
    diffusivity,
    region_map,
    region_owner,
):
    levels, rows_lat, rows_lon = courant_x.shape
    cells = rows_lat * rows_lon
    lon_count = lax.axis_size("lon")
    lat_count = lax.axis_size("lat")
    devices = lon_count * lat_count
    per_device = sounding_misfit.shape[0]
    capacity = max(2, 3 * per_device // (2 * devices))
    regions = region_owner.shape[0]
    slots = jnp.arange(per_device, dtype=jnp.int32)
    valid = slots < sounding_count[0]
    owner = sounding_owner[:, 0]
    earlier = (
        (owner[:, None] == owner[None, :]) & (slots[:, None] < slots[None, :]) & valid[:, None]
    )
    rank = jnp.sum(earlier.astype(jnp.int32), axis=0)
    spill = devices * capacity
    target = jnp.where(valid, owner * capacity + rank, spill)
    forcing = sounding_misfit[:, None] * sounding_kernel.T
    code = (sounding_step * cells + sounding_cell).astype(jnp.float32)
    send_rows = jax.ops.segment_sum(forcing, target, num_segments=spill + 1)[:spill]
    send_code = jax.ops.segment_sum(code, target, num_segments=spill + 1)[:spill]
    send_rows = send_rows.reshape(lon_count, lat_count, capacity * levels)
    send_code = send_code.reshape(lon_count, lat_count, capacity)
    got_rows, got_code = (
        lax.all_to_all(
            lax.all_to_all(send_rows, "lon", split_axis=0, concat_axis=0, tiled=True),
            "lat",
            split_axis=1,
            concat_axis=1,
            tiled=True,
        ),
        lax.all_to_all(
            lax.all_to_all(send_code, "lon", split_axis=0, concat_axis=0, tiled=True),
            "lat",
            split_axis=1,
            concat_axis=1,
            tiled=True,
        ),
    )
    got_rows = got_rows.reshape(devices * capacity, levels)
    got_code = got_code.reshape(-1).astype(jnp.int32)
    deposit = jax.ops.segment_sum(got_rows, got_code, num_segments=STEPS * cells)
    deposit = (
        deposit.reshape(STEPS, cells, levels)
        .transpose(0, 2, 1)
        .reshape(STEPS, levels, rows_lat, rows_lon)
    )
    field = jnp.zeros((levels, rows_lat, rows_lon), jnp.float32)
    surfaces = []
    for step in range(STEPS):
        field = field + deposit[step]
        padded = with_halo(field, (("lon", 2), ("lat", 1)), 1)
        padded = padded * lat_mask(rows_lat, 1)
        field = diffuse(advect(padded, courant_x, courant_y), diffusivity)
        surfaces.append(field[0])
    positions = region_owner[region_map].reshape(-1)

    def region_partial(surface):
        return jax.ops.segment_sum(surface.reshape(-1), positions, num_segments=regions)

    partial_all = jnp.stack([region_partial(surface) for surface in surfaces])
    totals = lax.psum_scatter(partial_all, ("lon", "lat"), scatter_dimension=1, tiled=True)
    return (field, totals)


MESH = pl.DeviceIdType.MESH
F32 = jnp.float32
BF16 = jnp.bfloat16
I32 = jnp.int32


def iota(shape, dim):
    return lax.broadcasted_iota(I32, shape, dim)


def one_hot(test, dtype=BF16):
    return jnp.where(test, 1.0, 0.0).astype(dtype)


def split(x):
    high = x.astype(BF16)
    return high, (x - high.astype(F32)).astype(BF16)


def dot_nt(a, b):
    return lax.dot_general(a, b, (((1,), (1,)), ((), ())), preferred_element_type=F32)


def kernel(
    lat_count,
    devices,
    sk_hbm,
    misfit_hbm,
    owner_hbm,
    cell_hbm,
    step_hbm,
    count_ref,
    cx_hbm,
    cy_hbm,
    dif_hbm,
    map_hbm,
    table_hbm,
    out_ref,
    reg_ref,
    sk_ref,
    misfit_ref,
    owner_ref,
    cell_ref,
    step_ref,
    cx_ref,
    cy_ref,
    dif_ref,
    map_ref,
    table_ref,
    load_sem,
    target,
    weights,
    send,
    got,
    dep0,
    dep1,
    base,
    inv,
    low,
    up,
    lon_out,
    lon_in,
    lat_out,
    lat_in,
    own_hot,
    loc_hot,
    part,
    part_in,
    a2a_send,
    a2a_recv,
    halo_send,
    halo_recv,
    reg_send,
    reg_recv,
):
    levels = cx_ref.shape[0]
    blocks = levels // 8
    planes = devices // 8
    half = devices * 16
    lon = lax.axis_index("lon")
    lat = lax.axis_index("lat")
    lon_count = devices // lat_count
    me = lon * lat_count + lat

    def flips(value, size):
        digits = [(value // (1 << k)) % 2 for k in range(size.bit_length() - 1)]
        return [
            sum((1 - d if mask >> k & 1 else d) * (1 << k) for k, d in enumerate(digits))
            for mask in range(size)
        ]

    lons = flips(lon, lon_count)
    lats = flips(lat, lat_count)

    def place(mask):
        return (lons[mask // lat_count], lats[mask % lat_count])

    def number(mask):
        return lons[mask // lat_count] * lat_count + lats[mask % lat_count]

    loads = {}
    for n, (name, src, dst) in enumerate(
        (
            ("owner", owner_hbm, owner_ref),
            ("misfit", misfit_hbm, misfit_ref),
            ("cell", cell_hbm, cell_ref),
            ("step", step_hbm, step_ref),
            ("sk", sk_hbm, sk_ref),
            ("dif", dif_hbm, dif_ref),
            ("map", map_hbm, map_ref),
            ("table", table_hbm, table_ref),
            ("cx", cx_hbm, cx_ref),
            ("cy", cy_hbm, cy_ref),
        )
    ):
        loads[name] = pltpu.make_async_copy(src, dst, load_sem.at[n])
        loads[name].start()
    barrier = pltpu.get_barrier_semaphore()

    for mask in range(1, devices):
        pl.semaphore_signal(barrier, inc=1, device_id=place(mask), device_id_type=MESH)

    loads["owner"].wait()
    lane1 = iota((1, 128), 1)
    owner_iota = iota((devices, 128), 0)
    hots, valids, owners = [], [], []
    count = count_ref[0]
    for c in range(8):
        valid = (lane1 + c * 128) < count
        row = owner_ref[c : c + 1, :]
        hots.append(one_hot(jnp.where(valid, row, -1) == owner_iota, F32))
        valids.append(valid)
        owners.append(row)
    earlier = one_hot((iota((128, 256), 0) < iota((128, 256), 1)))
    ranks = jnp.dot(
        jnp.concatenate(hots, axis=0).astype(BF16), earlier, preferred_element_type=F32
    )
    carry = jnp.zeros((devices, 128), F32)
    for c in range(8):
        part_c = ranks[c * devices : (c + 1) * devices]
        rank = jnp.sum(hots[c] * (part_c[:, :128] + carry), axis=0, keepdims=True).astype(I32)
        carry = carry + part_c[:, 128:]
        spot = (rank // 16) * half + owners[c] * 16 + rank % 16
        target[c : c + 1, :] = jnp.where(valids[c], spot, -1)

    for name in ("misfit", "cell", "step", "sk"):
        loads[name].wait()
    for c in range(8):
        at = slice(c * 128, (c + 1) * 128)
        forcing = sk_ref[:, at] * misfit_ref[c : c + 1, :]
        code = (step_ref[c : c + 1, :] * 1024 + cell_ref[c : c + 1, :]).astype(F32)
        code = jnp.broadcast_to(code, (8, 128))
        for h in range(2):
            if h == 0:
                rest = forcing[:40]
            else:
                rest = jnp.concatenate([forcing[40:], jnp.zeros((8, 128), F32)], axis=0)
            high, small = split(jnp.concatenate([forcing, code, rest, code], axis=0))
            weights[h, 0:128, at] = high
            weights[h, 128:256, at] = small

    sub128 = iota((128, 128), 0)
    lane128 = iota((128, 128), 1)
    order = [2, 3, 1, 0]
    arrival = [0, 1, 3, 2]

    def select_rows(first):
        return jnp.concatenate(
            [one_hot(target[c : c + 1, :] - first == sub128) for c in range(8)], axis=1
        )

    for x in order:
        there = number(x * 8) // 8
        rows = pl.ds(pl.multiple_of(there * 128, 128), 128)
        late = select_rows(2 * half + there * 128)
        for h in range(2):
            picks = jnp.concatenate([select_rows(h * half + there * 128), late], axis=0)
            both = dot_nt(picks, weights[h])
            both = both[:, :128] + both[:, 128:]
            send[h, rows, :] = jnp.where(lane128 < 80, both[:128], both[128:])

        if x == order[0]:
            pl.semaphore_wait(barrier, devices - 1)
        for mask in range(max(1, x * 8), x * 8 + 8):
            peer = number(mask)
            pltpu.make_async_remote_copy(
                src_ref=send.at[:, pl.ds(pl.multiple_of(peer * 16, 16), 16), :],
                dst_ref=got.at[:, pl.ds(pl.multiple_of(me * 16, 16), 16), :],
                send_sem=a2a_send.at[x],
                recv_sem=a2a_recv.at[x],
                device_id=place(mask),
                device_id_type=MESH,
            ).start()
    mine = pl.ds(pl.multiple_of(me * 16, 16), 16)
    got[:, mine, :] = send[:, mine, :]

    def factor(b, carry):
        k_prev, up_prev = carry
        for i in range(8):
            row = pl.ds(pl.multiple_of(b * 64 + i * 8, 8), 8)
            k_now = dif_ref[b * 8 + i]
            r = 1.0 / ((1.0 + k_prev + k_now) - k_prev * up_prev)
            inv[row, :] = r
            low[row, :] = k_prev * r
            up_prev = k_now * r
            up[row, :] = up_prev
            k_prev = k_now
        return (k_prev, up_prev)

    zero = jnp.zeros((8, 128), F32)
    loads["dif"].wait()
    lax.fori_loop(0, blocks, factor, (zero, zero))

    loads["map"].wait()
    loads["table"].wait()
    table = table_ref[...]
    table = jnp.concatenate([table // 128, table % 128], axis=0).astype(F32).astype(BF16)
    for a in range(8):
        at = slice(a * 128, (a + 1) * 128)
        region = map_ref[a : a + 1, :]
        found = jnp.dot(table, one_hot(region % 128 == sub128), preferred_element_type=F32)
        pick = one_hot(region // 128 == owner_iota, F32)
        own = jnp.sum(found[:devices] * pick, axis=0, keepdims=True).astype(I32)
        loc = jnp.sum(found[devices:] * pick, axis=0, keepdims=True).astype(I32)
        own_hot[:, at] = one_hot(own == owner_iota, F32)
        loc_hot[:, at] = one_hot(loc == sub128)

    sub8 = iota((8, 128), 0)
    lane256 = iota((128, 256), 1)

    def spread(rows, code):
        mask = one_hot((code // 128) % 8 == sub8, F32)
        y = (rows[:, None, :] * mask[None]).reshape(levels * 8, 128)
        return split(y)

    def column(code):
        return one_hot(code % 128 + (code // 1024) * 128 == lane256)

    for n, x in enumerate(arrival):
        there = number(x * 8) // 8
        if x == 0:
            seen = got.at[:, pl.ds(0, 112), :]
        else:
            seen = got.at[:, pl.ds(0, 128), :]
        pltpu.make_async_copy(seen, seen, a2a_recv.at[x]).wait()
        rows = pl.ds(pl.multiple_of(there * 128, 128), 128)
        first = got[0, rows, :]
        second = got[1, rows, :]
        first_t = first.T
        second_t = second.T
        late_t = jnp.concatenate([first_t[80:120], second_t[80:112]], axis=0)
        left, right = [], []
        for values, code_row, code_col in (
            (first_t[:72], first_t[72:73], first[:, 72:73]),
            (second_t[:72], second_t[72:73], second[:, 72:73]),
            (late_t, first_t[120:121], first[:, 120:121]),
        ):
            left.extend(spread(values, code_row.astype(I32)))
            right.extend([column(code_col.astype(I32))] * 2)
        total = jnp.dot(
            jnp.concatenate(left, axis=1),
            jnp.concatenate(right, axis=0),
            preferred_element_type=F32,
        )
        if n == 0:
            dep0[...] = total[:, :128]
            dep1[...] = total[:, 128:]
        else:
            dep0[...] += total[:, :128]
            dep1[...] += total[:, 128:]

    lane8 = iota((8, 128), 1)
    east = ((lon + 1) % lon_count, lat)
    west = (lax.rem(lon + lon_count - 1, lon_count), lat)
    north = (lon, lax.rem(lat + 1, lat_count))
    south = (lon, lax.rem(lat + lat_count - 1, lat_count))
    has_south = (lat > 0).astype(F32)
    has_north = (lat < lat_count - 1).astype(F32)

    def region_part(surface, step):
        spread_rows = jnp.concatenate(
            [own_hot[:, a * 128 : (a + 1) * 128] * surface[a : a + 1] for a in range(8)], axis=1
        )
        both = dot_nt(jnp.concatenate(split(spread_rows), axis=0), loc_hot[...])
        total = both[:devices] + both[devices:]
        for o in range(devices):
            part[o, step : step + 1, :] = total[o : o + 1]

    loads["cx"].wait()
    loads["cy"].wait()
    surface = None
    for step in range(STEPS):
        def gather(n, carry):
            first, last = carry
            b = blocks - 1 - n
            first = pltpu.roll(first, 8, 1)
            last = pltpu.roll(last, 8, 1)
            for i in range(8):
                x = dep0[pl.ds(pl.multiple_of(b * 64 + i * 8, 8), 8), :]
                first = jnp.where(lane8 == i, pltpu.roll(x, i, 1) if i else x, first)
                last = jnp.where(lane8 == i, pltpu.roll(x, i + 1, 1), last)
            return (first, last)

        first, last = lax.fori_loop(0, blocks, gather, (zero, zero), unroll=True)
        lon_out[step, 0] = first
        lon_out[step, 1] = last
        lat_out[step, 0] = dep0[pl.ds(0, levels, stride=8), :]
        lat_out[step, 1] = dep0[pl.ds(7, levels, stride=8), :]
        copies = []
        for n, (src, dst, to) in enumerate(
            (
                (lat_out.at[step, 0], lat_in.at[step, 1], south),
                (lat_out.at[step, 1], lat_in.at[step, 0], north),
                (lon_out.at[step, 0], lon_in.at[step, 1], west),
                (lon_out.at[step, 1], lon_in.at[step, 0], east),
            )
        ):
            copy = pltpu.make_async_remote_copy(
                src_ref=src,
                dst_ref=dst,
                send_sem=halo_send.at[step, n],
                recv_sem=halo_recv.at[step, n],
                device_id=to,
                device_id_type=MESH,
            )
            copy.start()
            copies.append(copy)

        def inside(b, carry):
            for i in range(8):
                row = pl.ds(pl.multiple_of(b * 64 + i * 8, 8), 8)
                x = dep0[row, :]
                cx = cx_ref[b * 8 + i]
                cy = cy_ref[b * 8 + i]
                to_west = jnp.where(lane8 == 0, 0.0, pltpu.roll(x, 1, 1))
                to_east = jnp.where(lane8 == 127, 0.0, pltpu.roll(x, 127, 1))
                to_south = jnp.where(sub8 == 0, 0.0, pltpu.roll(x, 1, 0))
                to_north = jnp.where(sub8 == 7, 0.0, pltpu.roll(x, 7, 0))
                base[row, :] = (
                    x
                    - jnp.maximum(cx, 0.0) * (x - to_west)
                    - jnp.maximum(-cx, 0.0) * (x - to_east)
                    - jnp.maximum(cy, 0.0) * (x - to_south)
                    - jnp.maximum(-cy, 0.0) * (x - to_north)
                )
            return carry

        lax.fori_loop(0, blocks, inside, 0, unroll=True)
        if step > 0:
            region_part(surface, step - 1)
        for copy in copies:
            copy.wait()

        def forward(b, carry):
            g, from_west, from_east = carry
            eight = pl.ds(pl.multiple_of(b * 8, 8), 8)
            from_south = lat_in[step, 0, eight, :] * has_south
            from_north = lat_in[step, 1, eight, :] * has_north
            for i in range(8):
                row = pl.ds(pl.multiple_of(b * 64 + i * 8, 8), 8)
                cx = cx_ref[b * 8 + i]
                cy = cy_ref[b * 8 + i]
                w = pltpu.roll(from_west, 128 - i, 1) if i else from_west
                e = pltpu.roll(from_east, 127 - i, 1)
                x_edge = jnp.where(
                    lane8 == 0,
                    jnp.maximum(cx, 0.0) * w,
                    jnp.where(lane8 == 127, jnp.maximum(-cx, 0.0) * e, 0.0),
                )
                y_edge = jnp.where(
                    sub8 == 0,
                    jnp.maximum(cy, 0.0) * from_south[i : i + 1],
                    jnp.where(sub8 == 7, jnp.maximum(-cy, 0.0) * from_north[i : i + 1], 0.0),
                )
                rhs = base[row, :] + x_edge + y_edge
                g = rhs * inv[row, :] + low[row, :] * g
                base[row, :] = g
            return (g, pltpu.roll(from_west, 120, 1), pltpu.roll(from_east, 120, 1))

        edges = (zero, lon_in[step, 0], lon_in[step, 1])
        lax.fori_loop(0, blocks, forward, edges, unroll=True)

        def backward(n, x):
            b = blocks - 1 - n
            for i in reversed(range(8)):
                row = pl.ds(pl.multiple_of(b * 64 + i * 8, 8), 8)
                x = base[row, :] + up[row, :] * x
                if step < STEPS - 1:
                    dep0[row, :] = x + dep1[row, :]
                else:
                    out_ref[b * 8 + i] = x
            return x

        surface = lax.fori_loop(0, blocks, backward, zero, unroll=True)

    region_part(surface, STEPS - 1)

    for mask in reversed(range(1, devices)):
        pltpu.make_async_remote_copy(
            src_ref=part.at[number(mask)],
            dst_ref=part_in.at[me],
            send_sem=reg_send,
            recv_sem=reg_recv,
            device_id=place(mask),
            device_id_type=MESH,
        ).start()
    part_in[me] = part[me]
    others = part_in.at[pl.ds(0, devices - 1)]
    pltpu.make_async_copy(others, others, reg_recv).wait()
    reg_ref[...] = jnp.sum(part_in[...], axis=0)

    others = part.at[pl.ds(0, devices - 1)]
    pltpu.make_async_copy(others, others, reg_send).wait()
    for x in order:
        seen = send.at[:, pl.ds(0, 112 if x == 0 else 128), :]
        pltpu.make_async_copy(seen, seen, a2a_send.at[x]).wait()


def body(
    sounding_kernel,
    sounding_misfit,
    sounding_owner,
    sounding_cell,
    sounding_step,
    sounding_count,
    courant_x,
    courant_y,
    diffusivity,
    region_map,
    region_owner,
):
    levels, rows_lat, rows_lon = courant_x.shape
    lat_count = lax.axis_size("lat")
    devices = lat_count * lax.axis_size("lon")
    per_device = sounding_misfit.shape[0]
    capacity = max(2, 3 * per_device // (2 * devices))
    if (capacity, devices, levels, rows_lat, rows_lon, per_device) != (48, 32, 72, 8, 128, 1024):
        return general_body(
            sounding_kernel,
            sounding_misfit,
            sounding_owner,
            sounding_cell,
            sounding_step,
            sounding_count,
            courant_x,
            courant_y,
            diffusivity,
            region_map,
            region_owner,
        )
    vmem = pl.BlockSpec(memory_space=pltpu.VMEM)
    hbm = pl.BlockSpec(memory_space=pltpu.HBM)
    smem = pl.BlockSpec(memory_space=pltpu.SMEM)
    cells = (levels * rows_lat, rows_lon)
    return pl.pallas_call(
        functools.partial(kernel, lat_count, devices),
        out_shape=(
            jax.ShapeDtypeStruct(courant_x.shape, F32),
            jax.ShapeDtypeStruct((STEPS, 128), F32),
        ),
        in_specs=[hbm] * 5 + [smem] + [hbm] * 5,
        out_specs=(vmem, vmem),
        scratch_shapes=[
            pltpu.VMEM((levels, per_device), F32),
            pltpu.VMEM((8, 128), F32),
            pltpu.VMEM((8, 128), I32),
            pltpu.VMEM((8, 128), I32),
            pltpu.VMEM((8, 128), I32),
            pltpu.VMEM(courant_x.shape, F32),
            pltpu.VMEM(courant_x.shape, F32),
            pltpu.VMEM(courant_x.shape, F32),
            pltpu.VMEM((8, 128), I32),
            pltpu.VMEM((region_owner.shape[0] // 128, 128), I32),
            pltpu.SemaphoreType.DMA((10,)),
            pltpu.VMEM((8, 128), I32),
            pltpu.VMEM((2, 256, per_device), BF16),
            pltpu.VMEM((2, devices * 16, 128), F32),
            pltpu.VMEM((2, devices * 16, 128), F32),
            pltpu.VMEM(cells, F32),
            pltpu.VMEM(cells, F32),
            pltpu.VMEM(cells, F32),
            pltpu.VMEM(cells, F32),
            pltpu.VMEM(cells, F32),
            pltpu.VMEM(cells, F32),
            pltpu.VMEM((STEPS, 2, 8, 128), F32),
            pltpu.VMEM((STEPS, 2, 8, 128), F32),
            pltpu.VMEM((STEPS, 2, levels, 128), F32),
            pltpu.VMEM((STEPS, 2, levels, 128), F32),
            pltpu.VMEM((devices, 1024), F32),
            pltpu.VMEM((128, 1024), BF16),
            pltpu.VMEM((devices, STEPS, 128), F32),
            pltpu.VMEM((devices, STEPS, 128), F32),
            pltpu.SemaphoreType.DMA((4,)),
            pltpu.SemaphoreType.DMA((4,)),
            pltpu.SemaphoreType.DMA((STEPS, 4)),
            pltpu.SemaphoreType.DMA((STEPS, 4)),
            pltpu.SemaphoreType.DMA,
            pltpu.SemaphoreType.DMA,
        ],
        compiler_params=pltpu.CompilerParams(
            collective_id=0, has_side_effects=True, vmem_limit_bytes=56 * 1024 * 1024
        ),
    )(
        sounding_kernel,
        sounding_misfit.reshape(8, 128),
        sounding_owner.reshape(8, 128),
        sounding_cell.reshape(8, 128),
        sounding_step.reshape(8, 128),
        sounding_count,
        courant_x,
        courant_y,
        diffusivity,
        region_map,
        region_owner.reshape(-1, 128),
    )


def solution(mesh):
    placed = (
        P(None, ("lon", "lat")),
        P(("lon", "lat")),
        P(("lon", "lat"), None),
        P(("lon", "lat")),
        P(("lon", "lat")),
        P(("lon", "lat")),
        P(None, "lat", "lon"),
        P(None, "lat", "lon"),
        P(None, "lat", "lon"),
        P("lat", "lon"),
        P(),
    )
    return jax.shard_map(
        body,
        mesh=mesh,
        in_specs=placed,
        out_specs=(P(None, "lat", "lon"), P(None, ("lon", "lat"))),
        check_vma=False,
    )
```

```python
import functools

import jax
import jax.numpy as jnp
from jax import lax
from jax.experimental import pallas as pl
from jax.experimental.pallas import tpu as pltpu
from jax.sharding import PartitionSpec as P

STEPS = 2


def with_halo(x, sides, width):
    for axis, dim in sides:
        size, length = (lax.axis_size(axis), x.shape[dim])
        up = [(i, (i + 1) % size) for i in range(size)]
        down = [(j, i) for i, j in up]
        last = lax.slice_in_dim(x, length - width, length, axis=dim)
        leading = lax.slice_in_dim(x, 0, width, axis=dim)
        before = lax.ppermute(last, axis, up)
        after = lax.ppermute(leading, axis, down)
        x = jnp.concatenate([before, x, after], axis=dim)
    return x


def advect(padded, courant_x, courant_y):
    center = padded[:, 1:-1, 1:-1]
    west = padded[:, 1:-1, :-2]
    east = padded[:, 1:-1, 2:]
    south = padded[:, :-2, 1:-1]
    north = padded[:, 2:, 1:-1]
    return (
        center
        - jnp.maximum(courant_x, 0.0) * (center - west)
        - jnp.maximum(-courant_x, 0.0) * (center - east)
        - jnp.maximum(courant_y, 0.0) * (center - south)
        - jnp.maximum(-courant_y, 0.0) * (center - north)
    )


def diffuse(field, coupling):
    below = jnp.concatenate([jnp.zeros_like(coupling[:1]), coupling[:-1]], axis=0)
    middle = 1.0 + below + coupling

    def forward(carry, item):
        w_prev, g_prev = carry
        low, mid, upper, rhs = item
        denom = mid + low * w_prev
        w_now = -upper / denom
        g_now = (rhs + low * g_prev) / denom
        return ((w_now, g_now), (w_now, g_now))

    zero = jnp.zeros_like(field[0])
    _, (w_all, g_all) = lax.scan(forward, (zero, zero), (below, middle, coupling, field))

    def backward(x_next, item):
        w_now, g_now = item
        x_now = g_now - w_now * x_next
        return (x_now, x_now)

    _, solved = lax.scan(backward, zero, (w_all, g_all), reverse=True)
    return solved


def lat_mask(rows_lat, width):
    first = lax.axis_index("lat") * rows_lat - width
    inside = first + jnp.arange(rows_lat + 2 * width, dtype=jnp.int32)
    limit = rows_lat * lax.axis_size("lat")
    return ((inside >= 0) & (inside < limit)).astype(jnp.float32)[:, None]


def general_body(
    sounding_kernel,
    sounding_misfit,
    sounding_owner,
    sounding_cell,
    sounding_step,
    sounding_count,
    courant_x,
    courant_y,
    diffusivity,
    region_map,
    region_owner,
):
    levels, rows_lat, rows_lon = courant_x.shape
    cells = rows_lat * rows_lon
    lon_count = lax.axis_size("lon")
    lat_count = lax.axis_size("lat")
    devices = lon_count * lat_count
    per_device = sounding_misfit.shape[0]
    capacity = max(2, 3 * per_device // (2 * devices))
    regions = region_owner.shape[0]
    slots = jnp.arange(per_device, dtype=jnp.int32)
    valid = slots < sounding_count[0]
    owner = sounding_owner[:, 0]
    earlier = (
        (owner[:, None] == owner[None, :]) & (slots[:, None] < slots[None, :]) & valid[:, None]
    )
    rank = jnp.sum(earlier.astype(jnp.int32), axis=0)
    spill = devices * capacity
    target = jnp.where(valid, owner * capacity + rank, spill)
    forcing = sounding_misfit[:, None] * sounding_kernel.T
    code = (sounding_step * cells + sounding_cell).astype(jnp.float32)
    send_rows = jax.ops.segment_sum(forcing, target, num_segments=spill + 1)[:spill]
    send_code = jax.ops.segment_sum(code, target, num_segments=spill + 1)[:spill]
    send_rows = send_rows.reshape(lon_count, lat_count, capacity * levels)
    send_code = send_code.reshape(lon_count, lat_count, capacity)
    got_rows, got_code = (
        lax.all_to_all(
            lax.all_to_all(send_rows, "lon", split_axis=0, concat_axis=0, tiled=True),
            "lat",
            split_axis=1,
            concat_axis=1,
            tiled=True,
        ),
        lax.all_to_all(
            lax.all_to_all(send_code, "lon", split_axis=0, concat_axis=0, tiled=True),
            "lat",
            split_axis=1,
            concat_axis=1,
            tiled=True,
        ),
    )
    got_rows = got_rows.reshape(devices * capacity, levels)
    got_code = got_code.reshape(-1).astype(jnp.int32)
    deposit = jax.ops.segment_sum(got_rows, got_code, num_segments=STEPS * cells)
    deposit = (
        deposit.reshape(STEPS, cells, levels)
        .transpose(0, 2, 1)
        .reshape(STEPS, levels, rows_lat, rows_lon)
    )
    field = jnp.zeros((levels, rows_lat, rows_lon), jnp.float32)
    surfaces = []
    for step in range(STEPS):
        field = field + deposit[step]
        padded = with_halo(field, (("lon", 2), ("lat", 1)), 1)
        padded = padded * lat_mask(rows_lat, 1)
        field = diffuse(advect(padded, courant_x, courant_y), diffusivity)
        surfaces.append(field[0])
    positions = region_owner[region_map].reshape(-1)

    def region_partial(surface):
        return jax.ops.segment_sum(surface.reshape(-1), positions, num_segments=regions)

    partial_all = jnp.stack([region_partial(surface) for surface in surfaces])
    totals = lax.psum_scatter(partial_all, ("lon", "lat"), scatter_dimension=1, tiled=True)
    return (field, totals)


MESH = pl.DeviceIdType.MESH
F32 = jnp.float32
BF16 = jnp.bfloat16
I32 = jnp.int32


def iota(shape, dim):
    return lax.broadcasted_iota(I32, shape, dim)


def one_hot(test, dtype=BF16):
    return jnp.where(test, 1.0, 0.0).astype(dtype)


def split(x):
    high = x.astype(BF16)
    return high, (x - high.astype(F32)).astype(BF16)


def dot_nt(a, b):
    return lax.dot_general(a, b, (((1,), (1,)), ((), ())), preferred_element_type=F32)


def kernel(
    lat_count,
    devices,
    sk_hbm,
    misfit_hbm,
    owner_hbm,
    cell_hbm,
    step_hbm,
    count_ref,
    cx_hbm,
    cy_hbm,
    dif_hbm,
    map_hbm,
    table_hbm,
    out_hbm,
    reg_ref,
    sk_ref,
    misfit_ref,
    owner_ref,
    cell_ref,
    step_ref,
    cx_ref,
    cy_ref,
    dif_ref,
    map_ref,
    table_ref,
    load_sem,
    out_ref,
    out_sem,
    target,
    weights,
    send,
    got,
    dep0,
    dep1,
    base,
    inv,
    low,
    up,
    lon_out,
    lon_in,
    lat_out,
    lat_in,
    own_hot,
    loc_hot,
    part,
    part_in,
    a2a_send,
    a2a_recv,
    halo_send,
    halo_recv,
    reg_send,
    reg_recv,
):
    levels = cx_ref.shape[0]
    blocks = levels // 8
    planes = devices // 8
    half = devices * 16
    lon = lax.axis_index("lon")
    lat = lax.axis_index("lat")
    lon_count = devices // lat_count
    me = lon * lat_count + lat

    def flips(value, size):
        digits = [(value // (1 << k)) % 2 for k in range(size.bit_length() - 1)]
        return [
            sum((1 - d if mask >> k & 1 else d) * (1 << k) for k, d in enumerate(digits))
            for mask in range(size)
        ]

    lons = flips(lon, lon_count)
    lats = flips(lat, lat_count)

    def place(mask):
        return (lons[mask // lat_count], lats[mask % lat_count])

    def number(mask):
        return lons[mask // lat_count] * lat_count + lats[mask % lat_count]

    loads = {}
    for n, (name, src, dst) in enumerate(
        (
            ("owner", owner_hbm, owner_ref),
            ("misfit", misfit_hbm, misfit_ref),
            ("cell", cell_hbm, cell_ref),
            ("step", step_hbm, step_ref),
            ("sk", sk_hbm, sk_ref),
            ("dif", dif_hbm, dif_ref),
            ("map", map_hbm, map_ref),
            ("table", table_hbm, table_ref),
            ("cx", cx_hbm, cx_ref),
            ("cy", cy_hbm, cy_ref),
        )
    ):
        loads[name] = pltpu.make_async_copy(src, dst, load_sem.at[n])
        loads[name].start()
    barrier = pltpu.get_barrier_semaphore()

    for mask in range(1, devices):
        pl.semaphore_signal(barrier, inc=1, device_id=place(mask), device_id_type=MESH)

    loads["owner"].wait()
    lane1 = iota((1, 128), 1)
    owner_iota = iota((devices, 128), 0)
    hots, valids, owners = [], [], []
    count = count_ref[0]
    for c in range(8):
        valid = (lane1 + c * 128) < count
        row = owner_ref[c : c + 1, :]
        hots.append(one_hot(jnp.where(valid, row, -1) == owner_iota, F32))
        valids.append(valid)
        owners.append(row)
    earlier = one_hot((iota((128, 256), 0) < iota((128, 256), 1)))
    ranks = jnp.dot(
        jnp.concatenate(hots, axis=0).astype(BF16), earlier, preferred_element_type=F32
    )
    carry = jnp.zeros((devices, 128), F32)
    for c in range(8):
        part_c = ranks[c * devices : (c + 1) * devices]
        rank = jnp.sum(hots[c] * (part_c[:, :128] + carry), axis=0, keepdims=True).astype(I32)
        carry = carry + part_c[:, 128:]
        spot = (rank // 16) * half + owners[c] * 16 + rank % 16
        target[c : c + 1, :] = jnp.where(valids[c], spot, -1)

    for name in ("misfit", "cell", "step", "sk"):
        loads[name].wait()
    for c in range(8):
        at = slice(c * 128, (c + 1) * 128)
        forcing = sk_ref[:, at] * misfit_ref[c : c + 1, :]
        code = (step_ref[c : c + 1, :] * 1024 + cell_ref[c : c + 1, :]).astype(F32)
        code = jnp.broadcast_to(code, (8, 128))
        for h in range(2):
            if h == 0:
                rest = forcing[:40]
            else:
                rest = jnp.concatenate([forcing[40:], jnp.zeros((8, 128), F32)], axis=0)
            high, small = split(jnp.concatenate([forcing, code, rest, code], axis=0))
            weights[h, 0:128, at] = high
            weights[h, 128:256, at] = small

    sub128 = iota((128, 128), 0)
    lane128 = iota((128, 128), 1)
    order = [2, 3, 0, 1]
    arrival = [0, 1, 3, 2]

    def select_rows(first):
        return jnp.concatenate(
            [one_hot(target[c : c + 1, :] - first == sub128) for c in range(8)], axis=1
        )

    for x in order:
        there = number(x * 8) // 8
        rows = pl.ds(pl.multiple_of(there * 128, 128), 128)
        late = select_rows(2 * half + there * 128)
        for h in range(2):
            picks = jnp.concatenate([select_rows(h * half + there * 128), late], axis=0)
            both = dot_nt(picks, weights[h])
            both = both[:, :128] + both[:, 128:]
            send[h, rows, :] = jnp.where(lane128 < 80, both[:128], both[128:])

        if x == order[0]:
            pl.semaphore_wait(barrier, devices - 1)
        for mask in range(max(1, x * 8), x * 8 + 8):
            peer = number(mask)
            pltpu.make_async_remote_copy(
                src_ref=send.at[:, pl.ds(pl.multiple_of(peer * 16, 16), 16), :],
                dst_ref=got.at[:, pl.ds(pl.multiple_of(me * 16, 16), 16), :],
                send_sem=a2a_send.at[x],
                recv_sem=a2a_recv.at[x],
                device_id=place(mask),
                device_id_type=MESH,
            ).start()
    mine = pl.ds(pl.multiple_of(me * 16, 16), 16)
    got[:, mine, :] = send[:, mine, :]

    def factor(b, carry):
        k_prev, up_prev = carry
        for i in range(8):
            row = pl.ds(pl.multiple_of(b * 64 + i * 8, 8), 8)
            k_now = dif_ref[b * 8 + i]
            r = 1.0 / ((1.0 + k_prev + k_now) - k_prev * up_prev)
            inv[row, :] = r
            low[row, :] = k_prev * r
            up_prev = k_now * r
            up[row, :] = up_prev
            k_prev = k_now
        return (k_prev, up_prev)

    zero = jnp.zeros((8, 128), F32)
    loads["dif"].wait()
    lax.fori_loop(0, blocks, factor, (zero, zero))

    loads["map"].wait()
    loads["table"].wait()
    table = table_ref[...]
    table = jnp.concatenate([table // 128, table % 128], axis=0).astype(F32).astype(BF16)
    for a in range(8):
        at = slice(a * 128, (a + 1) * 128)
        region = map_ref[a : a + 1, :]
        found = jnp.dot(table, one_hot(region % 128 == sub128), preferred_element_type=F32)
        pick = one_hot(region // 128 == owner_iota, F32)
        own = jnp.sum(found[:devices] * pick, axis=0, keepdims=True).astype(I32)
        loc = jnp.sum(found[devices:] * pick, axis=0, keepdims=True).astype(I32)
        own_hot[:, at] = one_hot(own == owner_iota, F32)
        loc_hot[:, at] = one_hot(loc == sub128)

    sub8 = iota((8, 128), 0)
    lane256 = iota((128, 256), 1)

    def spread(rows, code):
        mask = one_hot((code // 128) % 8 == sub8, F32)
        y = (rows[:, None, :] * mask[None]).reshape(levels * 8, 128)
        return split(y)

    def column(code):
        return one_hot(code % 128 + (code // 1024) * 128 == lane256)

    for n, x in enumerate(arrival):
        there = number(x * 8) // 8
        if x == 0:
            seen = got.at[:, pl.ds(0, 112), :]
        else:
            seen = got.at[:, pl.ds(0, 128), :]
        pltpu.make_async_copy(seen, seen, a2a_recv.at[x]).wait()
        rows = pl.ds(pl.multiple_of(there * 128, 128), 128)
        first = got[0, rows, :]
        second = got[1, rows, :]
        first_t = first.T
        second_t = second.T
        late_t = jnp.concatenate([first_t[80:120], second_t[80:112]], axis=0)
        left, right = [], []
        for values, code_row, code_col in (
            (first_t[:72], first_t[72:73], first[:, 72:73]),
            (second_t[:72], second_t[72:73], second[:, 72:73]),
            (late_t, first_t[120:121], first[:, 120:121]),
        ):
            left.extend(spread(values, code_row.astype(I32)))
            right.extend([column(code_col.astype(I32))] * 2)
        total = jnp.dot(
            jnp.concatenate(left, axis=1),
            jnp.concatenate(right, axis=0),
            preferred_element_type=F32,
        )
        if n == 0:
            dep0[...] = total[:, :128]
            dep1[...] = total[:, 128:]
        else:
            dep0[...] += total[:, :128]
            dep1[...] += total[:, 128:]

    lane8 = iota((8, 128), 1)
    east = ((lon + 1) % lon_count, lat)
    west = (lax.rem(lon + lon_count - 1, lon_count), lat)
    north = (lon, lax.rem(lat + 1, lat_count))
    south = (lon, lax.rem(lat + lat_count - 1, lat_count))
    has_south = (lat > 0).astype(F32)
    has_north = (lat < lat_count - 1).astype(F32)

    def region_part(surface, step):
        spread_rows = jnp.concatenate(
            [own_hot[:, a * 128 : (a + 1) * 128] * surface[a : a + 1] for a in range(8)], axis=1
        )
        both = dot_nt(jnp.concatenate(split(spread_rows), axis=0), loc_hot[...])
        total = both[:devices] + both[devices:]
        for o in range(devices):
            part[o, step : step + 1, :] = total[o : o + 1]

    loads["cx"].wait()
    loads["cy"].wait()
    surface = None
    for step in range(STEPS):
        def gather(n, carry):
            first, last = carry
            b = blocks - 1 - n
            first = pltpu.roll(first, 8, 1)
            last = pltpu.roll(last, 8, 1)
            for i in range(8):
                x = dep0[pl.ds(pl.multiple_of(b * 64 + i * 8, 8), 8), :]
                first = jnp.where(lane8 == i, pltpu.roll(x, i, 1) if i else x, first)
                last = jnp.where(lane8 == i, pltpu.roll(x, i + 1, 1), last)
            return (first, last)

        first, last = lax.fori_loop(0, blocks, gather, (zero, zero), unroll=True)
        lon_out[step, 0] = first
        lon_out[step, 1] = last
        lat_out[step, 0] = dep0[pl.ds(0, levels, stride=8), :]
        lat_out[step, 1] = dep0[pl.ds(7, levels, stride=8), :]
        copies = []
        for n, (src, dst, to) in enumerate(
            (
                (lat_out.at[step, 0], lat_in.at[step, 1], south),
                (lat_out.at[step, 1], lat_in.at[step, 0], north),
                (lon_out.at[step, 0], lon_in.at[step, 1], west),
                (lon_out.at[step, 1], lon_in.at[step, 0], east),
            )
        ):
            copy = pltpu.make_async_remote_copy(
                src_ref=src,
                dst_ref=dst,
                send_sem=halo_send.at[step, n],
                recv_sem=halo_recv.at[step, n],
                device_id=to,
                device_id_type=MESH,
            )
            copy.start()
            copies.append(copy)

        def inside(b, carry):
            for i in range(8):
                row = pl.ds(pl.multiple_of(b * 64 + i * 8, 8), 8)
                x = dep0[row, :]
                cx = cx_ref[b * 8 + i]
                cy = cy_ref[b * 8 + i]
                to_west = jnp.where(lane8 == 0, 0.0, pltpu.roll(x, 1, 1))
                to_east = jnp.where(lane8 == 127, 0.0, pltpu.roll(x, 127, 1))
                to_south = jnp.where(sub8 == 0, 0.0, pltpu.roll(x, 1, 0))
                to_north = jnp.where(sub8 == 7, 0.0, pltpu.roll(x, 7, 0))
                base[row, :] = (
                    x
                    - jnp.maximum(cx, 0.0) * (x - to_west)
                    - jnp.maximum(-cx, 0.0) * (x - to_east)
                    - jnp.maximum(cy, 0.0) * (x - to_south)
                    - jnp.maximum(-cy, 0.0) * (x - to_north)
                )
            return carry

        lax.fori_loop(0, blocks, inside, 0, unroll=True)
        if step > 0:
            region_part(surface, step - 1)
        for copy in copies:
            copy.wait()

        def forward(b, carry):
            g, from_west, from_east = carry
            eight = pl.ds(pl.multiple_of(b * 8, 8), 8)
            from_south = lat_in[step, 0, eight, :] * has_south
            from_north = lat_in[step, 1, eight, :] * has_north
            for i in range(8):
                row = pl.ds(pl.multiple_of(b * 64 + i * 8, 8), 8)
                cx = cx_ref[b * 8 + i]
                cy = cy_ref[b * 8 + i]
                w = pltpu.roll(from_west, 128 - i, 1) if i else from_west
                e = pltpu.roll(from_east, 127 - i, 1)
                x_edge = jnp.where(
                    lane8 == 0,
                    jnp.maximum(cx, 0.0) * w,
                    jnp.where(lane8 == 127, jnp.maximum(-cx, 0.0) * e, 0.0),
                )
                y_edge = jnp.where(
                    sub8 == 0,
                    jnp.maximum(cy, 0.0) * from_south[i : i + 1],
                    jnp.where(sub8 == 7, jnp.maximum(-cy, 0.0) * from_north[i : i + 1], 0.0),
                )
                rhs = base[row, :] + x_edge + y_edge
                g = rhs * inv[row, :] + low[row, :] * g
                base[row, :] = g
            return (g, pltpu.roll(from_west, 120, 1), pltpu.roll(from_east, 120, 1))

        edges = (zero, lon_in[step, 0], lon_in[step, 1])
        lax.fori_loop(0, blocks, forward, edges, unroll=True)

        def backward(n, x):
            b = blocks - 1 - n
            for i in reversed(range(8)):
                row = pl.ds(pl.multiple_of(b * 64 + i * 8, 8), 8)
                x = base[row, :] + up[row, :] * x
                if step < STEPS - 1:
                    dep0[row, :] = x + dep1[row, :]
                else:
                    out_ref[b * 8 + i] = x
            return x

        surface = lax.fori_loop(0, blocks, backward, zero, unroll=True)

    result = pltpu.make_async_copy(out_ref, out_hbm, out_sem)
    result.start()
    region_part(surface, STEPS - 1)

    for mask in reversed(range(1, devices)):
        pltpu.make_async_remote_copy(
            src_ref=part.at[number(mask)],
            dst_ref=part_in.at[me],
            send_sem=reg_send,
            recv_sem=reg_recv,
            device_id=place(mask),
            device_id_type=MESH,
        ).start()
    part_in[me] = part[me]
    others = part_in.at[pl.ds(0, devices - 1)]
    pltpu.make_async_copy(others, others, reg_recv).wait()
    reg_ref[...] = jnp.sum(part_in[...], axis=0)

    result.wait()
    others = part.at[pl.ds(0, devices - 1)]
    pltpu.make_async_copy(others, others, reg_send).wait()
    for x in order:
        seen = send.at[:, pl.ds(0, 112 if x == 0 else 128), :]
        pltpu.make_async_copy(seen, seen, a2a_send.at[x]).wait()


def body(
    sounding_kernel,
    sounding_misfit,
    sounding_owner,
    sounding_cell,
    sounding_step,
    sounding_count,
    courant_x,
    courant_y,
    diffusivity,
    region_map,
    region_owner,
):
    levels, rows_lat, rows_lon = courant_x.shape
    lat_count = lax.axis_size("lat")
    devices = lat_count * lax.axis_size("lon")
    per_device = sounding_misfit.shape[0]
    capacity = max(2, 3 * per_device // (2 * devices))
    if (capacity, devices, levels, rows_lat, rows_lon, per_device) != (48, 32, 72, 8, 128, 1024):
        return general_body(
            sounding_kernel,
            sounding_misfit,
            sounding_owner,
            sounding_cell,
            sounding_step,
            sounding_count,
            courant_x,
            courant_y,
            diffusivity,
            region_map,
            region_owner,
        )
    vmem = pl.BlockSpec(memory_space=pltpu.VMEM)
    hbm = pl.BlockSpec(memory_space=pltpu.HBM)
    smem = pl.BlockSpec(memory_space=pltpu.SMEM)
    cells = (levels * rows_lat, rows_lon)
    return pl.pallas_call(
        functools.partial(kernel, lat_count, devices),
        out_shape=(
            jax.ShapeDtypeStruct(courant_x.shape, F32),
            jax.ShapeDtypeStruct((STEPS, 128), F32),
        ),
        in_specs=[hbm] * 5 + [smem] + [hbm] * 5,
        out_specs=(hbm, vmem),
        scratch_shapes=[
            pltpu.VMEM((levels, per_device), F32),
            pltpu.VMEM((8, 128), F32),
            pltpu.VMEM((8, 128), I32),
            pltpu.VMEM((8, 128), I32),
            pltpu.VMEM((8, 128), I32),
            pltpu.VMEM(courant_x.shape, F32),
            pltpu.VMEM(courant_x.shape, F32),
            pltpu.VMEM(courant_x.shape, F32),
            pltpu.VMEM((8, 128), I32),
            pltpu.VMEM((region_owner.shape[0] // 128, 128), I32),
            pltpu.SemaphoreType.DMA((10,)),
            pltpu.VMEM(courant_x.shape, F32),
            pltpu.SemaphoreType.DMA,
            pltpu.VMEM((8, 128), I32),
            pltpu.VMEM((2, 256, per_device), BF16),
            pltpu.VMEM((2, devices * 16, 128), F32),
            pltpu.VMEM((2, devices * 16, 128), F32),
            pltpu.VMEM(cells, F32),
            pltpu.VMEM(cells, F32),
            pltpu.VMEM(cells, F32),
            pltpu.VMEM(cells, F32),
            pltpu.VMEM(cells, F32),
            pltpu.VMEM(cells, F32),
            pltpu.VMEM((STEPS, 2, 8, 128), F32),
            pltpu.VMEM((STEPS, 2, 8, 128), F32),
            pltpu.VMEM((STEPS, 2, levels, 128), F32),
            pltpu.VMEM((STEPS, 2, levels, 128), F32),
            pltpu.VMEM((devices, 1024), F32),
            pltpu.VMEM((128, 1024), BF16),
            pltpu.VMEM((devices, STEPS, 128), F32),
            pltpu.VMEM((devices, STEPS, 128), F32),
            pltpu.SemaphoreType.DMA((4,)),
            pltpu.SemaphoreType.DMA((4,)),
            pltpu.SemaphoreType.DMA((STEPS, 4)),
            pltpu.SemaphoreType.DMA((STEPS, 4)),
            pltpu.SemaphoreType.DMA,
            pltpu.SemaphoreType.DMA,
        ],
        compiler_params=pltpu.CompilerParams(
            collective_id=0, has_side_effects=True, vmem_limit_bytes=56 * 1024 * 1024
        ),
    )(
        sounding_kernel,
        sounding_misfit.reshape(8, 128),
        sounding_owner.reshape(8, 128),
        sounding_cell.reshape(8, 128),
        sounding_step.reshape(8, 128),
        sounding_count,
        courant_x,
        courant_y,
        diffusivity,
        region_map,
        region_owner.reshape(-1, 128),
    )


def solution(mesh):
    placed = (
        P(None, ("lon", "lat")),
        P(("lon", "lat")),
        P(("lon", "lat"), None),
        P(("lon", "lat")),
        P(("lon", "lat")),
        P(("lon", "lat")),
        P(None, "lat", "lon"),
        P(None, "lat", "lon"),
        P(None, "lat", "lon"),
        P("lat", "lon"),
        P(),
    )
    return jax.shard_map(
        body,
        mesh=mesh,
        in_specs=placed,
        out_specs=(P(None, "lat", "lon"), P(None, ("lon", "lat"))),
        check_vma=False,
    )
```
